32 devices in a mesh: replica: 2 (over y), gx: 8 (over z, x), gy: 2 (over core).
Axes of the slice: x: 2, y: 2, z: 4, core: 2. Of those that a mesh axis runs over, the one named last changes fastest.
Arguments:
- hidden: bfloat16 [16, 8192], P(('replica', 'gx')), parts along dimension 0, may hold values from -6 to 6
- exit_layer: int32 [2], P('replica'), parts along dimension 0, may hold values from 0 to 79
- norm_gains: bfloat16 [80, 8192], P(None, 'gx'), may hold values from 0.099609375 to 1.8984375
- w_query: bfloat16 [8192, 8192], P('gx', 'gy'), may hold values from -0.0625 to 0.0625
- key_weight: bfloat16 [8192, 1024], P('gx', 'gy'), may hold values from -0.0625 to 0.0625
- value_weight: bfloat16 [8192, 1024], P('gx', 'gy'), may hold values from -0.0625 to 0.0625
- w_out: bfloat16 [8192, 8192], P('gy', 'gx'), may hold values from -0.0625 to 0.0625
- key_cache: bfloat16 [16, 8, 512, 128], P(('replica', 'gx'), 'gy'), parts along dimension 0
- cached_value_rows: bfloat16 [16, 8, 512, 128], P(('replica', 'gx'), 'gy'), parts along dimension 0, may hold values from -6 to 6
- lengths: int32 [16], P(('replica', 'gx')), parts along dimension 0, may hold values from 1 to 512, as said below
Outputs:
- layer_out: bfloat16 [16, 8192], P('replica', 'gx'), parts along dimension 0
The draws below stay inside these ranges and needn't reach their ends.
There are 2 independent parts, one for each index of `replica`. The reference program is written for one: setup_inputs(seed, part) draws one part's arguments, and reference() takes and returns one part's arrays. A program takes and returns all parts, laid end to end along the dimension named above; an argument that names none is the same for every part. Nothing has to cross between parts.
Inputs may be any that keep to these rules, and one draw needn't show every extreme that they name: Slots 0 to lengths[r] - 1 of row r are filled; the new token sits at position lengths[r].
All inputs are finite; a program needn't handle non-finite values.
Results may differ from the reference program's by a relative error of at most 0.012.
The reference program's roundings to bfloat16 on the way (of `normed`, `probs` and `attn`) count: a program that leaves them out, or rounds other values in their place, can miss the bound.
Values may be sent and summed in bfloat16 or wider, within the bound.
A program may use at most 64 MiB of HBM per device.

```python
import math
import jax
import jax.numpy as jnp
from jax import lax

MODEL_WIDTH = 8192
HQ = 64
KEY_VALUE_HEADS = 8
HEAD_SIZE = 128
LAYERS = 80
CACHE_SLOTS = 512
GROUP_ROWS = 8


def draw_key_cache(key, part):
    key = jax.random.fold_in(key, 11)
    array_shape = (GROUP_ROWS, KEY_VALUE_HEADS, CACHE_SLOTS, HEAD_SIZE)
    values = jnp.clip(jax.random.normal(key, array_shape, jnp.float32) * 2.5, -15.0, 15.0)
    return values.astype(jnp.bfloat16)


def draw_lengths(key, part):
    key = jax.random.fold_in(key, 23)
    first, second = jax.random.split(key)
    filled = jax.random.randint(first, (GROUP_ROWS,), 1, CACHE_SLOTS + 1, dtype=jnp.int32)
    picks = jax.random.permutation(second, GROUP_ROWS)
    filled = filled.at[picks[0]].set(CACHE_SLOTS)
    filled = filled.at[picks[1]].set(1)
    return filled


def levels(own_key, shape, cuts, least, top_value):
    level, own = 1.0, jax.random.fold_in(own_key, 6)
    for dim, parts in cuts:
        steps = jnp.exp(jax.random.uniform(jax.random.fold_in(own, dim), (parts,), jnp.float32, least / len(cuts), top_value / len(cuts)))
        level = level * jnp.repeat(steps, shape[dim] // parts).reshape([-1 if axis == dim else 1 for axis in range(len(shape))])
    return level


def bell_draw(own_key, dims, scale, limit, shards=(), kind=jnp.bfloat16):
    entries = scale * jax.random.normal(own_key, dims, jnp.float32)
    if shards:
        entries = entries * levels(own_key, dims, shards, -0.22, 0.18)
    return jnp.clip(entries, -limit, limit).astype(kind)


def setup_inputs(seed: int = 0, part: int = 0) -> dict:
    arg_keys = jax.random.split(jax.random.key(seed), 11)
    part_splits = jax.random.split(jax.random.fold_in(arg_keys[10], part), 11)
    return {
        "hidden": bell_draw(part_splits[0], (GROUP_ROWS, MODEL_WIDTH), 1.0, 6.0, ((0, 8),)),
        "exit_layer": jax.random.randint(part_splits[1], (1,), 0, LAYERS).astype(jnp.int32),
        "norm_gains": jnp.clip(1.0 + 0.18 * jax.random.normal(arg_keys[2], (LAYERS, MODEL_WIDTH), jnp.float32), 0.099609375, 1.8984375).astype(jnp.bfloat16),
        "w_query": bell_draw(arg_keys[3], (MODEL_WIDTH, HQ * HEAD_SIZE), MODEL_WIDTH ** -0.5, 0.0625, ((0, 8), (1, 2))),
        "key_weight": bell_draw(arg_keys[4], (MODEL_WIDTH, KEY_VALUE_HEADS * HEAD_SIZE), MODEL_WIDTH ** -0.5, 0.0625, ((0, 8), (1, 2))),
        "value_weight": bell_draw(arg_keys[5], (MODEL_WIDTH, KEY_VALUE_HEADS * HEAD_SIZE), MODEL_WIDTH ** -0.5, 0.0625, ((0, 8), (1, 2))),
        "w_out": bell_draw(arg_keys[6], (HQ * HEAD_SIZE, MODEL_WIDTH), (HQ * HEAD_SIZE) ** -0.5, 0.0625, ((0, 2), (1, 8))),
        "key_cache": draw_key_cache(jax.random.fold_in(jax.random.fold_in(arg_keys[10], part), 71), part),
        "cached_value_rows": bell_draw(part_splits[8], (GROUP_ROWS, KEY_VALUE_HEADS, CACHE_SLOTS, HEAD_SIZE), 1.0, 6.0, ((0, 8), (1, 2))),
        "lengths": draw_lengths(jax.random.fold_in(jax.random.fold_in(arg_keys[10], part), 71), part),
    }


def rotate(vectors, positions):
    half = vectors.shape[-1] // 2
    steps = jnp.arange(half, dtype=jnp.float32) * (2.0 / vectors.shape[-1])
    freqs = jnp.exp(-math.log(500000.0) * steps)
    angles = positions[:, None, None] * freqs[None, None, :]
    cosine = jnp.cos(angles)
    sine = jnp.sin(angles)
    first = vectors[..., :half]
    second = vectors[..., half:]
    return jnp.concatenate([first * cosine - second * sine, second * cosine + first * sine], axis=-1)

def reference(hidden, exit_layer, norm_gains, w_query, key_weight, value_weight, w_out, key_cache, cached_value_rows, lengths):
    rows = hidden.shape[0]
    head = key_cache.shape[3]
    kv_heads = key_cache.shape[1]
    q_heads = w_query.shape[1] // head
    group = q_heads // kv_heads
    x32 = hidden.astype(jnp.float32)
    inv = lax.rsqrt(lax.optimization_barrier(jnp.mean(x32 * x32, axis=-1, keepdims=True)) + 1e-05)
    gain = lax.dynamic_index_in_dim(norm_gains, exit_layer[0], 0, keepdims=False).astype(jnp.float32)
    normed = (x32 * inv * gain[None, :]).astype(jnp.bfloat16)
    query = jnp.dot(normed, w_query, preferred_element_type=jnp.float32)
    keys = jnp.dot(normed, key_weight, preferred_element_type=jnp.float32)
    values = jnp.dot(normed, value_weight, preferred_element_type=jnp.float32)
    positions = lengths.astype(jnp.float32)
    rq = rotate(query.reshape(rows, q_heads, head), positions).astype(jnp.bfloat16)
    rk = rotate(keys.reshape(rows, kv_heads, head), positions).astype(jnp.bfloat16)
    nv = values.reshape(rows, kv_heads, head).astype(jnp.bfloat16)
    scale = 1.0 / math.sqrt(head)
    grouped = rq.astype(jnp.float32).reshape(rows, kv_heads, group, head)
    scores = jnp.einsum('rgqd,rgpd->rgqp', grouped, key_cache.astype(jnp.float32)) * scale
    own = jnp.einsum('rgqd,rgd->rgq', grouped, rk.astype(jnp.float32)) * scale
    valid = jnp.arange(key_cache.shape[2], dtype=jnp.int32)[None, :] < lengths[:, None]
    scores = jnp.where(valid[:, None, None, :], scores, -1e+30)
    top = jnp.maximum(lax.optimization_barrier(jnp.max(scores, axis=-1)), own)
    weights = jnp.where(valid[:, None, None, :], jnp.exp(scores - top[..., None]), 0.0)
    own_weight = jnp.exp(own - top)
    total = lax.optimization_barrier(jnp.sum(weights, axis=-1)) + own_weight
    probs = (weights / total[..., None]).astype(jnp.bfloat16)
    own_prob = (own_weight / total).astype(jnp.bfloat16)
    attn = jnp.einsum('rgqp,rgpd->rgqd', probs.astype(jnp.float32), cached_value_rows.astype(jnp.float32))
    attn = attn + own_prob.astype(jnp.float32)[..., None] * nv.astype(jnp.float32)[:, :, None, :]
    attn = attn.reshape(rows, q_heads * head).astype(jnp.bfloat16)
    return (x32 + jnp.dot(attn, w_out, preferred_element_type=jnp.float32)).astype(jnp.bfloat16)
```

```python
import functools
import math

import jax
import jax.numpy as jnp
from jax import lax
from jax.experimental import pallas as pl
from jax.experimental.pallas import tpu as pltpu
from jax.sharding import PartitionSpec as P

MESH = pl.DeviceIdType.MESH
LANES = 128
QUERY_PIECES = 4
OUT_PIECES = 2


def kernel(
    gx,
    hidden_ref,
    layer_ref,
    length_ref,
    gains_hbm,
    wq_hbm,
    wk_hbm,
    wv_hbm,
    wo_hbm,
    kc_hbm,
    vc_hbm,
    out_ref,
    gains_ref,
    wq_ref,
    wk_ref,
    wv_ref,
    wo_ref,
    kc_ref,
    vc_ref,
    x_send,
    x_recv,
    p_send,
    p_recv,
    a_send,
    a_recv,
    y_send,
    y_recv,
    local_sems,
    x_sems,
    p_sems,
    a_sems,
    y_sems,
):
    me = lax.axis_index("gx")
    core = lax.axis_index("gy")
    other = 1 - core
    peers = [lax.rem(me + d, gx) for d in range(1, gx)]
    cols = x_recv.shape[2] - LANES
    kv_local, slots, head = kc_ref.shape
    q_local = wq_ref.shape[1] // head
    group = q_local // kv_local

    barrier = pltpu.get_barrier_semaphore()
    for peer in peers:
        pl.semaphore_signal(barrier, inc=1, device_id={"gx": peer}, device_id_type=MESH)
    pl.semaphore_signal(barrier, inc=1, device_id={"gy": other}, device_id_type=MESH)

    width = wq_ref.shape[1] // QUERY_PIECES
    pairs = [(gains_hbm, gains_ref)]
    for i in range(QUERY_PIECES):
        piece = pl.ds(i * width, width)
        pairs.append((wq_hbm.at[:, piece], wq_ref.at[:, piece]))
    pairs += [(wk_hbm, wk_ref), (wv_hbm, wv_ref), (kc_hbm.at[0], kc_ref), (vc_hbm.at[0], vc_ref)]
    out_width = wo_ref.shape[1] // OUT_PIECES
    for i in range(OUT_PIECES):
        piece = pl.ds(i * out_width, out_width)
        pairs.append((wo_hbm.at[:, piece], wo_ref.at[:, piece]))
    loads = [
        pltpu.make_async_copy(src, dst, local_sems.at[i]) for i, (src, dst) in enumerate(pairs)
    ]
    for load in loads:
        load.start()

    def exchange(src, dst, sems):
        copies = [
            pltpu.make_async_remote_copy(
                src_ref=src(peer),
                dst_ref=dst.at[me],
                send_sem=sems.at[0, peer],
                recv_sem=sems.at[1, me],
                device_id={"gx": peer},
                device_id_type=MESH,
            )
            for peer in peers
        ]
        for copy in copies:
            copy.start()
        return copies

    def arrive(src, dst, sems):
        for peer in peers:
            pltpu.make_async_remote_copy(
                src_ref=src(peer),
                dst_ref=dst.at[peer],
                send_sem=sems.at[0, peer],
                recv_sem=sems.at[1, peer],
                device_id={"gx": peer},
                device_id_type=MESH,
            ).wait_recv()

    row = hidden_ref[...].astype(jnp.float32)
    inv_row = lax.rsqrt(jnp.mean(row * row, axis=-1, keepdims=True) + 1e-05)
    inv_lanes = jnp.broadcast_to(inv_row, (1, LANES))
    for j in range(gx):
        x_send[j, :, :cols] = row[:, j * cols : (j + 1) * cols]
        x_send[j, :, cols:] = inv_lanes
    x_recv[me] = x_send[me]
    pl.semaphore_wait(barrier, gx)
    x_copies = exchange(lambda peer: x_send.at[peer], x_recv, x_sems)

    half = head // 2
    lane = lax.broadcasted_iota(jnp.int32, (1, head), 1)
    index = jnp.where(lane < half, lane, lane - half).astype(jnp.float32)
    freqs = jnp.exp(-math.log(500000.0) * (index * (2.0 / head)))
    length = length_ref[0]
    angles = length.astype(jnp.float32) * freqs
    cosine = jnp.cos(angles)
    sine = jnp.sin(angles)
    sine = jnp.where(lane < half, -sine, sine)

    loads[0].wait()
    table = gains_ref[...].astype(jnp.float32)
    chosen = lax.broadcasted_iota(jnp.int32, table.shape, 0) == layer_ref[0]
    gain = jnp.sum(jnp.where(chosen, table, 0.0), axis=0, keepdims=True)

    arrive(lambda peer: x_send.at[peer], x_recv, x_sems)
    x32 = x_recv[:, 0, :cols]
    inv = x_recv[:, 0, cols : cols + 1]
    normed = (x32 * inv * gain).astype(jnp.bfloat16)

    def project(weights, first):
        sums = jnp.dot(normed, weights, preferred_element_type=jnp.float32)
        for h in range(sums.shape[1] // head):
            p_send[:, first + h, :] = sums[:, h * head : (h + 1) * head]

    for i in range(QUERY_PIECES):
        loads[1 + i].wait()
        project(wq_ref[:, i * width : (i + 1) * width], i * width // head)
    loads[1 + QUERY_PIECES].wait()
    project(wk_ref[...], q_local)
    loads[2 + QUERY_PIECES].wait()
    project(wv_ref[...], q_local + kv_local)
    p_copies = exchange(lambda peer: p_send.at[peer], p_recv, p_sems)
    p_recv[me] = p_send[me]
    loads[3 + QUERY_PIECES].wait()
    loads[4 + QUERY_PIECES].wait()
    arrive(lambda peer: p_send.at[peer], p_recv, p_sems)
    total = p_recv[0]
    for j in range(1, gx):
        total = total + p_recv[j]

    rotated = total * cosine + pltpu.roll(total, half, 1) * sine
    scale = 1.0 / math.sqrt(head)
    valid = lax.broadcasted_iota(jnp.int32, (1, slots), 1) < length
    for g in range(kv_local):
        rq = rotated[g * group : (g + 1) * group].astype(jnp.bfloat16)
        rk = rotated[q_local + g : q_local + g + 1].astype(jnp.bfloat16).astype(jnp.float32)
        first = q_local + kv_local + g
        nv = total[first : first + 1].astype(jnp.bfloat16).astype(jnp.float32)
        scores = (
            lax.dot_general(
                rq, kc_ref[g], (((1,), (1,)), ((), ())), preferred_element_type=jnp.float32
            )
            * scale
        )
        own = jnp.sum(rq.astype(jnp.float32) * rk, axis=-1, keepdims=True) * scale
        scores = jnp.where(valid, scores, -1e30)
        top = jnp.maximum(jnp.max(scores, axis=-1, keepdims=True), own)
        exps = jnp.where(valid, jnp.exp(scores - top), 0.0)
        own_exp = jnp.exp(own - top)
        denominator = jnp.sum(exps, axis=-1, keepdims=True) + own_exp
        probs = (exps / denominator).astype(jnp.bfloat16)
        own_prob = (own_exp / denominator).astype(jnp.bfloat16).astype(jnp.float32)
        attn = jnp.dot(probs, vc_ref[g], preferred_element_type=jnp.float32) + own_prob * nv
        a_send[g * group : (g + 1) * group, :] = attn.astype(jnp.bfloat16).astype(jnp.float32)
    a_copies = exchange(lambda peer: a_send, a_recv, a_sems)
    a_recv[me] = a_send[...]
    for i in range(OUT_PIECES):
        loads[5 + QUERY_PIECES + i].wait()
    arrive(lambda peer: a_send, a_recv, a_sems)
    attended = jnp.concatenate([a_recv[:, h, :] for h in range(q_local)], axis=1).astype(
        jnp.bfloat16
    )
    y_copies = []
    for i in range(OUT_PIECES):
        piece = slice(i * out_width, (i + 1) * out_width)
        y_send[i] = jnp.dot(attended, wo_ref[:, piece], preferred_element_type=jnp.float32)
        copy = pltpu.make_async_remote_copy(
            src_ref=y_send.at[i],
            dst_ref=y_recv.at[i],
            send_sem=y_sems.at[0, i],
            recv_sem=y_sems.at[1, i],
            device_id={"gy": other},
            device_id_type=MESH,
        )
        copy.start()
        y_copies.append(copy)
    for i in range(OUT_PIECES):
        y_copies[i].wait_recv()
        piece = slice(i * out_width, (i + 1) * out_width)
        summed = y_send[i] + y_recv[i]
        out_ref[:, piece] = (x_recv[:, 0, piece] + summed).astype(out_ref.dtype)
    for copy in x_copies + p_copies + a_copies + y_copies:
        copy.wait_send()


def fused(
    hidden,
    exit_layer,
    norm_gains,
    w_query,
    key_weight,
    value_weight,
    w_out,
    key_cache,
    cached_value_rows,
    lengths,
):
    gx = lax.axis_size("gx")
    cols = norm_gains.shape[1]
    _, kv_local, slots, head = key_cache.shape
    q_local = w_query.shape[1] // head
    heads = q_local + 2 * kv_local
    f32, bf16 = jnp.float32, jnp.bfloat16
    vmem = pl.BlockSpec(memory_space=pltpu.VMEM)
    smem = pl.BlockSpec(memory_space=pltpu.SMEM)
    anywhere = pl.BlockSpec(memory_space=pl.ANY)
    dma = pltpu.SemaphoreType.DMA
    weights = w_query.size + key_weight.size + value_weight.size + w_out.size
    return pl.pallas_call(
        functools.partial(kernel, gx),
        out_shape=jax.ShapeDtypeStruct((gx, cols), bf16),
        in_specs=[vmem, smem, smem] + [anywhere] * 7,
        out_specs=vmem,
        scratch_shapes=[
            pltpu.VMEM(norm_gains.shape, bf16),
            pltpu.VMEM(w_query.shape, bf16),
            pltpu.VMEM(key_weight.shape, bf16),
            pltpu.VMEM(value_weight.shape, bf16),
            pltpu.VMEM(w_out.shape, bf16),
            pltpu.VMEM(key_cache.shape[1:], bf16),
            pltpu.VMEM(key_cache.shape[1:], bf16),
            pltpu.VMEM((gx, 1, cols + LANES), f32),
            pltpu.VMEM((gx, 1, cols + LANES), f32),
            pltpu.VMEM((gx, heads, head), f32),
            pltpu.VMEM((gx, heads, head), f32),
            pltpu.VMEM((q_local, head), f32),
            pltpu.VMEM((gx, q_local, head), f32),
            pltpu.VMEM((OUT_PIECES, gx, cols // OUT_PIECES), f32),
            pltpu.VMEM((OUT_PIECES, gx, cols // OUT_PIECES), f32),
            dma((5 + QUERY_PIECES + OUT_PIECES,)),
            dma((2, gx)),
            dma((2, gx)),
            dma((2, gx)),
            dma((2, OUT_PIECES)),
        ],
        compiler_params=pltpu.CompilerParams(
            collective_id=0, has_side_effects=True, vmem_limit_bytes=56 * 2**20
        ),
        cost_estimate=pl.CostEstimate(
            flops=2 * gx * weights, bytes_accessed=2 * weights, transcendentals=0
        ),
    )(
        hidden,
        exit_layer,
        lengths,
        norm_gains,
        w_query,
        key_weight,
        value_weight,
        w_out,
        key_cache,
        cached_value_rows,
    )


def rotate(vectors, positions):
    half = vectors.shape[-1] // 2
    steps = jnp.arange(half, dtype=jnp.float32) * (2.0 / vectors.shape[-1])
    freqs = jnp.exp(-math.log(500000.0) * steps)
    angles = positions[:, None, None] * freqs[None, None, :]
    cosine = jnp.cos(angles)
    sine = jnp.sin(angles)
    first = vectors[..., :half]
    second = vectors[..., half:]
    return jnp.concatenate(
        [first * cosine - second * sine, second * cosine + first * sine], axis=-1
    )


def body(
    hidden,
    exit_layer,
    norm_gains,
    w_query,
    key_weight,
    value_weight,
    w_out,
    key_cache,
    cached_value_rows,
    lengths,
):
    rows_dev = hidden.shape[0]
    head = key_cache.shape[3]
    kv_local = key_cache.shape[1]
    q_local = w_query.shape[1] // head
    group = q_local // kv_local
    columns = lax.all_to_all(hidden, "gx", split_axis=1, concat_axis=0, tiled=True)
    x32 = columns.astype(jnp.float32)
    own_rows = hidden.astype(jnp.float32)
    inv_local = lax.rsqrt(jnp.mean(own_rows * own_rows, axis=-1) + 1e-05)
    inv = lax.all_gather(inv_local, "gx", axis=0, tiled=True)
    gain = lax.dynamic_index_in_dim(norm_gains, exit_layer[0], 0, keepdims=False).astype(
        jnp.float32
    )
    normed = (x32 * inv[:, None] * gain[None, :]).astype(jnp.bfloat16)
    weights = jnp.concatenate([w_query, key_weight, value_weight], axis=1)
    width_q = w_query.shape[1]
    width_k = key_weight.shape[1]
    partial_sums = jnp.dot(normed, weights, preferred_element_type=jnp.float32)
    shares = lax.psum_scatter(partial_sums, "gx", scatter_dimension=1, tiled=True)
    projected = lax.all_to_all(shares, "gx", split_axis=0, concat_axis=1, tiled=True)
    query = projected[:, :width_q]
    keys = projected[:, width_q : width_q + width_k]
    values = projected[:, width_q + width_k :]
    positions = lengths.astype(jnp.float32)
    rq = rotate(query.reshape(rows_dev, q_local, head), positions).astype(jnp.bfloat16)
    rk = rotate(keys.reshape(rows_dev, kv_local, head), positions).astype(jnp.bfloat16)
    nv = values.reshape(rows_dev, kv_local, head).astype(jnp.bfloat16)
    scale = 1.0 / math.sqrt(head)
    grouped = rq.reshape(rows_dev, kv_local, group, head)
    scores = (
        jnp.einsum("rgqd,rgpd->rgqp", grouped, key_cache, preferred_element_type=jnp.float32)
        * scale
    )
    own = jnp.einsum("rgqd,rgd->rgq", grouped, rk, preferred_element_type=jnp.float32) * scale
    valid = jnp.arange(key_cache.shape[2], dtype=jnp.int32)[None, :] < lengths[:, None]
    scores = jnp.where(valid[:, None, None, :], scores, -1e30)
    top = jnp.maximum(jnp.max(scores, axis=-1), own)
    weights_exp = jnp.where(valid[:, None, None, :], jnp.exp(scores - top[..., None]), 0.0)
    own_weight = jnp.exp(own - top)
    total = jnp.sum(weights_exp, axis=-1) + own_weight
    probs = (weights_exp / total[..., None]).astype(jnp.bfloat16)
    own_prob = (own_weight / total).astype(jnp.bfloat16)
    attn = jnp.einsum(
        "rgqp,rgpd->rgqd", probs, cached_value_rows, preferred_element_type=jnp.float32
    )
    attn = attn + own_prob.astype(jnp.float32)[..., None] * nv.astype(jnp.float32)[:, :, None, :]
    attn = attn.reshape(rows_dev, q_local * head).astype(jnp.bfloat16)
    mixed = jnp.dot(
        lax.all_gather(attn, "gx", axis=0, tiled=True), w_out, preferred_element_type=jnp.float32
    )
    summed = lax.psum(mixed, "gy")
    return (x32 + summed).astype(jnp.bfloat16)


def step(*arrays):
    hidden, gains = arrays[0], arrays[2]
    if gains.shape[1] % (LANES * OUT_PIECES) == 0 and hidden.shape[0] == 1:
        return fused(*arrays)
    return body(*arrays)


def solution(mesh):
    placed = (
        P(("replica", "gx"), None),
        P("replica"),
        P(None, "gx"),
        P("gx", "gy"),
        P("gx", "gy"),
        P("gx", "gy"),
        P("gy", "gx"),
        P(("replica", "gx"), "gy", None, None),
        P(("replica", "gx"), "gy", None, None),
        P(("replica", "gx")),
    )
    return jax.shard_map(
        step, mesh=mesh, in_specs=placed, out_specs=P("replica", "gx"), check_vma=False
    )
```

```python
import functools
import math

import jax
import jax.numpy as jnp
from jax import lax
from jax.experimental import pallas as pl
from jax.experimental.pallas import tpu as pltpu
from jax.sharding import PartitionSpec as P

MESH = pl.DeviceIdType.MESH
LANES = 128
OUT_PIECES = 2


def kernel(
    gx,
    hidden_ref,
    ints_ref,
    gains_hbm,
    wq_hbm,
    wk_hbm,
    wv_hbm,
    wo_hbm,
    kc_hbm,
    vc_hbm,
    out_ref,
    gains_ref,
    wq_ref,
    wk_ref,
    wv_ref,
    wo_ref,
    kc_ref,
    vc_ref,
    x_send,
    x_recv,
    p_send,
    p_recv,
    a_send,
    a_recv,
    a_wide,
    y_send,
    y_recv,
    local_sems,
    x_sems,
    p_sems,
    a_sems,
    y_sems,
):
    me = lax.axis_index("gx")
    core = lax.axis_index("gy")
    other = 1 - core
    peers = [lax.rem(me + d, gx) for d in range(1, gx)]
    cols = x_recv.shape[2] - LANES
    kv_local, slots, head = kc_ref.shape
    q_local = wq_ref.shape[1] // head
    group = q_local // kv_local

    barrier = pltpu.get_barrier_semaphore()
    for peer in peers:
        pl.semaphore_signal(barrier, inc=1, device_id={"gx": peer}, device_id_type=MESH)
    pl.semaphore_signal(barrier, inc=1, device_id={"gy": other}, device_id_type=MESH)

    width = wq_ref.shape[1] // kv_local
    depth = wo_ref.shape[0] // OUT_PIECES
    pairs = [(gains_hbm, gains_ref)]
    pairs += [(wk_hbm, wk_ref), (wv_hbm, wv_ref)]
    for i in range(kv_local):
        piece = pl.ds(i * width, width)
        pairs.append((wq_hbm.at[:, piece], wq_ref.at[:, piece]))
    pairs += [(kc_hbm.at[0], kc_ref), (vc_hbm.at[0], vc_ref)]
    for i in range(OUT_PIECES):
        piece = pl.ds(i * depth, depth)
        pairs.append((wo_hbm.at[piece], wo_ref.at[piece]))
    loads = [
        pltpu.make_async_copy(src, dst, local_sems.at[i]) for i, (src, dst) in enumerate(pairs)
    ]
    for load in loads:
        load.start()

    def descriptor(src, dst, sems, peer, owner):
        return pltpu.make_async_remote_copy(
            src_ref=src(peer),
            dst_ref=dst(owner),
            send_sem=sems.at[0, peer],
            recv_sem=sems.at[1, owner],
            device_id={"gx": peer},
            device_id_type=MESH,
        )

    def exchange(src, dst, sems):
        copies = [descriptor(src, dst, sems, peer, me) for peer in peers]
        for copy in copies:
            copy.start()
        return copies

    def arrive(src, dst, sems):
        for peer in peers:
            descriptor(src, dst, sems, peer, peer).wait_recv()

    row = hidden_ref[...].astype(jnp.float32)
    inv_row = lax.rsqrt(jnp.mean(row * row, axis=-1, keepdims=True) + 1e-05)
    inv_lanes = jnp.broadcast_to(inv_row, (1, LANES))
    for j in range(gx):
        x_send[j, :, :cols] = row[:, j * cols : (j + 1) * cols]
        x_send[j, :, cols:] = inv_lanes
    x_recv[me] = x_send[me]
    pl.semaphore_wait(barrier, gx)
    x_route = (lambda peer: x_send.at[peer], lambda peer: x_recv.at[peer], x_sems)
    copies = exchange(*x_route)

    half = head // 2
    lane = lax.broadcasted_iota(jnp.int32, (1, head), 1)
    index = jnp.where(lane < half, lane, lane - half).astype(jnp.float32)
    freqs = jnp.exp(-math.log(500000.0) * (index * (2.0 / head)))
    length = ints_ref[:, 1:]
    angles = length.astype(jnp.float32) * freqs
    cosine = jnp.cos(angles)
    sine = jnp.sin(angles)
    sine = jnp.where(lane < half, -sine, sine)

    loads[0].wait()
    table = gains_ref[...].astype(jnp.float32)
    chosen = lax.broadcasted_iota(jnp.int32, table.shape, 0) == ints_ref[:, :1]
    gain = jnp.sum(jnp.where(chosen, table, 0.0), axis=0, keepdims=True)

    arrive(*x_route)
    x32 = x_recv[:, 0, :cols]
    inv = x_recv[:, 0, cols : cols + 1]
    normed = (x32 * inv * gain).astype(jnp.bfloat16)

    def project(weights, first):
        sums = jnp.dot(normed, weights, preferred_element_type=jnp.float32)
        for h in range(sums.shape[1] // head):
            p_send[:, first + h, :] = sums[:, h * head : (h + 1) * head]

    def p_route(first, count, sems):
        rows = pl.ds(first, count)
        return lambda peer: p_send.at[peer, rows], lambda peer: p_recv.at[peer, rows], sems

    def summed_rows(first, count):
        rows = slice(first, first + count)
        total = p_recv[0, rows]
        for j in range(1, gx):
            total = total + p_recv[j, rows]
        return total

    def turn(total):
        return total * cosine + pltpu.roll(total, half, 1) * sine

    early = 2 * kv_local + group
    late = (kv_local - 1) * group
    early_route = p_route(0, early, p_sems.at[0])
    late_route = p_route(early, late, p_sems.at[1])
    loads[1].wait()
    project(wk_ref[...], 0)
    loads[2].wait()
    project(wv_ref[...], kv_local)
    loads[3].wait()
    project(wq_ref[:, :width], 2 * kv_local)
    copies += exchange(*early_route)
    for i in range(1, kv_local):
        loads[3 + i].wait()
        project(wq_ref[:, i * width : (i + 1) * width], 2 * kv_local + i * group)
    copies += exchange(*late_route)
    p_recv[me] = p_send[me]
    loads[3 + kv_local].wait()
    loads[4 + kv_local].wait()
    arrive(*early_route)
    fresh = summed_rows(0, early)
    turned = turn(fresh)

    scale = 1.0 / math.sqrt(head)
    valid = lax.broadcasted_iota(jnp.int32, (1, slots), 1) < length

    def attend(g, rotated):
        rq = rotated.astype(jnp.bfloat16)
        rk = turned[g : g + 1].astype(jnp.bfloat16).astype(jnp.float32)
        nv = fresh[kv_local + g : kv_local + g + 1].astype(jnp.bfloat16).astype(jnp.float32)
        scores = (
            lax.dot_general(
                rq, kc_ref[g], (((1,), (1,)), ((), ())), preferred_element_type=jnp.float32
            )
            * scale
        )
        own = jnp.sum(rq.astype(jnp.float32) * rk, axis=-1, keepdims=True) * scale
        scores = jnp.where(valid, scores, -1e30)
        top = jnp.maximum(jnp.max(scores, axis=-1, keepdims=True), own)
        exps = jnp.where(valid, jnp.exp(scores - top), 0.0)
        own_exp = jnp.exp(own - top)
        denominator = jnp.sum(exps, axis=-1, keepdims=True) + own_exp
        probs = (exps / denominator).astype(jnp.bfloat16)
        own_prob = (own_exp / denominator).astype(jnp.bfloat16).astype(jnp.float32)
        return jnp.dot(probs, vc_ref[g], preferred_element_type=jnp.float32) + own_prob * nv

    attn = [attend(0, turned[2 * kv_local :])]
    arrive(*late_route)
    queries = turn(summed_rows(early, late))
    span = q_local // OUT_PIECES
    groups = kv_local // OUT_PIECES
    a_routes = []
    for i in range(OUT_PIECES):
        while len(attn) < (i + 1) * groups:
            g = len(attn)
            attn.append(attend(g, queries[(g - 1) * group : g * group]))
        piece = jnp.concatenate(attn[i * groups : (i + 1) * groups], axis=0)
        piece = piece.astype(jnp.bfloat16)
        a_send[i] = piece
        route = (
            lambda peer, i=i: a_send.at[i],
            lambda peer, i=i: a_recv.at[i, peer],
            a_sems.at[i],
        )
        copies += exchange(*route)
        a_recv[i, me] = piece
        a_routes.append(route)
    out_width = wo_ref.shape[1] // OUT_PIECES
    total = None
    for i in range(OUT_PIECES):
        loads[5 + kv_local + i].wait()
        arrive(*a_routes[i])
        a_wide[i] = a_recv[i].astype(jnp.float32)
        attended = jnp.concatenate([a_wide[i, :, h, :] for h in range(span)], axis=1)
        attended = attended.astype(jnp.bfloat16)
        rows = slice(i * depth, (i + 1) * depth)
        if i < OUT_PIECES - 1:
            term = jnp.dot(attended, wo_ref[rows], preferred_element_type=jnp.float32)
            total = term if total is None else total + term
    y_copies = []
    for i in range(OUT_PIECES):
        piece = slice(i * out_width, (i + 1) * out_width)
        term = jnp.dot(attended, wo_ref[rows, piece], preferred_element_type=jnp.float32)
        y_send[i] = total[:, piece] + term
        copy = pltpu.make_async_remote_copy(
            src_ref=y_send.at[i],
            dst_ref=y_recv.at[i],
            send_sem=y_sems.at[0, i],
            recv_sem=y_sems.at[1, i],
            device_id={"gy": other},
            device_id_type=MESH,
        )
        copy.start()
        y_copies.append(copy)
    for i in range(OUT_PIECES):
        y_copies[i].wait_recv()
        piece = slice(i * out_width, (i + 1) * out_width)
        summed = y_send[i] + y_recv[i]
        out_ref[:, piece] = (x_recv[:, 0, piece] + summed).astype(out_ref.dtype)
    for copy in copies + y_copies:
        copy.wait_send()


def fused(
    hidden,
    exit_layer,
    norm_gains,
    w_query,
    key_weight,
    value_weight,
    w_out,
    key_cache,
    cached_value_rows,
    lengths,
):
    gx = lax.axis_size("gx")
    cols = norm_gains.shape[1]
    _, kv_local, slots, head = key_cache.shape
    q_local = w_query.shape[1] // head
    heads = q_local + 2 * kv_local
    f32, bf16 = jnp.float32, jnp.bfloat16
    vmem = pl.BlockSpec(memory_space=pltpu.VMEM)
    anywhere = pl.BlockSpec(memory_space=pl.ANY)
    dma = pltpu.SemaphoreType.DMA
    weights = w_query.size + key_weight.size + value_weight.size + w_out.size
    return pl.pallas_call(
        functools.partial(kernel, gx),
        out_shape=jax.ShapeDtypeStruct((gx, cols), bf16),
        in_specs=[vmem, vmem] + [anywhere] * 7,
        out_specs=vmem,
        scratch_shapes=[
            pltpu.VMEM(norm_gains.shape, bf16),
            pltpu.VMEM(w_query.shape, bf16),
            pltpu.VMEM(key_weight.shape, bf16),
            pltpu.VMEM(value_weight.shape, bf16),
            pltpu.VMEM(w_out.shape, bf16),
            pltpu.VMEM(key_cache.shape[1:], bf16),
            pltpu.VMEM(key_cache.shape[1:], bf16),
            pltpu.VMEM((gx, 1, cols + LANES), f32),
            pltpu.VMEM((gx, 1, cols + LANES), f32),
            pltpu.VMEM((gx, heads, head), f32),
            pltpu.VMEM((gx, heads, head), f32),
            pltpu.VMEM((OUT_PIECES, q_local // OUT_PIECES, head), bf16),
            pltpu.VMEM((OUT_PIECES, gx, q_local // OUT_PIECES, head), bf16),
            pltpu.VMEM((OUT_PIECES, gx, q_local // OUT_PIECES, head), f32),
            pltpu.VMEM((OUT_PIECES, gx, cols // OUT_PIECES), f32),
            pltpu.VMEM((OUT_PIECES, gx, cols // OUT_PIECES), f32),
            dma((5 + kv_local + OUT_PIECES,)),
            dma((2, gx)),
            dma((2, 2, gx)),
            dma((OUT_PIECES, 2, gx)),
            dma((2, OUT_PIECES)),
        ],
        compiler_params=pltpu.CompilerParams(
            collective_id=0, has_side_effects=True, vmem_limit_bytes=56 * 2**20
        ),
        cost_estimate=pl.CostEstimate(
            flops=2 * gx * weights, bytes_accessed=2 * weights, transcendentals=0
        ),
    )(
        hidden,
        jnp.concatenate([exit_layer, lengths])[None, :],
        norm_gains,
        w_query,
        key_weight,
        value_weight,
        w_out,
        key_cache,
        cached_value_rows,
    )


def rotate(vectors, positions):
    half = vectors.shape[-1] // 2
    steps = jnp.arange(half, dtype=jnp.float32) * (2.0 / vectors.shape[-1])
    freqs = jnp.exp(-math.log(500000.0) * steps)
    angles = positions[:, None, None] * freqs[None, None, :]
    cosine = jnp.cos(angles)
    sine = jnp.sin(angles)
    first = vectors[..., :half]
    second = vectors[..., half:]
    return jnp.concatenate(
        [first * cosine - second * sine, second * cosine + first * sine], axis=-1
    )


def body(
    hidden,
    exit_layer,
    norm_gains,
    w_query,
    key_weight,
    value_weight,
    w_out,
    key_cache,
    cached_value_rows,
    lengths,
):
    rows_dev = hidden.shape[0]
    head = key_cache.shape[3]
    kv_local = key_cache.shape[1]
    q_local = w_query.shape[1] // head
    group = q_local // kv_local
    columns = lax.all_to_all(hidden, "gx", split_axis=1, concat_axis=0, tiled=True)
    x32 = columns.astype(jnp.float32)
    own_rows = hidden.astype(jnp.float32)
    inv_local = lax.rsqrt(jnp.mean(own_rows * own_rows, axis=-1) + 1e-05)
    inv = lax.all_gather(inv_local, "gx", axis=0, tiled=True)
    gain = lax.dynamic_index_in_dim(norm_gains, exit_layer[0], 0, keepdims=False).astype(
        jnp.float32
    )
    normed = (x32 * inv[:, None] * gain[None, :]).astype(jnp.bfloat16)
    weights = jnp.concatenate([w_query, key_weight, value_weight], axis=1)
    width_q = w_query.shape[1]
    width_k = key_weight.shape[1]
    partial_sums = jnp.dot(normed, weights, preferred_element_type=jnp.float32)
    shares = lax.psum_scatter(partial_sums, "gx", scatter_dimension=1, tiled=True)
    projected = lax.all_to_all(shares, "gx", split_axis=0, concat_axis=1, tiled=True)
    query = projected[:, :width_q]
    keys = projected[:, width_q : width_q + width_k]
    values = projected[:, width_q + width_k :]
    positions = lengths.astype(jnp.float32)
    rq = rotate(query.reshape(rows_dev, q_local, head), positions).astype(jnp.bfloat16)
    rk = rotate(keys.reshape(rows_dev, kv_local, head), positions).astype(jnp.bfloat16)
    nv = values.reshape(rows_dev, kv_local, head).astype(jnp.bfloat16)
    scale = 1.0 / math.sqrt(head)
    grouped = rq.reshape(rows_dev, kv_local, group, head)
    scores = (
        jnp.einsum("rgqd,rgpd->rgqp", grouped, key_cache, preferred_element_type=jnp.float32)
        * scale
    )
    own = jnp.einsum("rgqd,rgd->rgq", grouped, rk, preferred_element_type=jnp.float32) * scale
    valid = jnp.arange(key_cache.shape[2], dtype=jnp.int32)[None, :] < lengths[:, None]
    scores = jnp.where(valid[:, None, None, :], scores, -1e30)
    top = jnp.maximum(jnp.max(scores, axis=-1), own)
    weights_exp = jnp.where(valid[:, None, None, :], jnp.exp(scores - top[..., None]), 0.0)
    own_weight = jnp.exp(own - top)
    total = jnp.sum(weights_exp, axis=-1) + own_weight
    probs = (weights_exp / total[..., None]).astype(jnp.bfloat16)
    own_prob = (own_weight / total).astype(jnp.bfloat16)
    attn = jnp.einsum(
        "rgqp,rgpd->rgqd", probs, cached_value_rows, preferred_element_type=jnp.float32
    )
    attn = attn + own_prob.astype(jnp.float32)[..., None] * nv.astype(jnp.float32)[:, :, None, :]
    attn = attn.reshape(rows_dev, q_local * head).astype(jnp.bfloat16)
    mixed = jnp.dot(
        lax.all_gather(attn, "gx", axis=0, tiled=True), w_out, preferred_element_type=jnp.float32
    )
    summed = lax.psum(mixed, "gy")
    return (x32 + summed).astype(jnp.bfloat16)


def step(*arrays):
    hidden, gains = arrays[0], arrays[2]
    if gains.shape[1] % (LANES * OUT_PIECES) == 0 and hidden.shape[0] == 1:
        return fused(*arrays)
    return body(*arrays)


def solution(mesh):
    placed = (
        P(("replica", "gx"), None),
        P("replica"),
        P(None, "gx"),
        P("gx", "gy"),
        P("gx", "gy"),
        P("gx", "gy"),
        P("gy", "gx"),
        P(("replica", "gx"), "gy", None, None),
        P(("replica", "gx"), "gy", None, None),
        P(("replica", "gx")),
    )
    return jax.shard_map(
        step, mesh=mesh, in_specs=placed, out_specs=P("replica", "gx"), check_vma=False
    )
```

```python
import functools
import math

import jax
import jax.numpy as jnp
from jax import lax
from jax.experimental import pallas as pl
from jax.experimental.pallas import tpu as pltpu
from jax.sharding import PartitionSpec as P

MESH = pl.DeviceIdType.MESH
LANES = 128
OUT_PIECES = 2


def kernel(
    gx,
    hidden_ref,
    layer_hbm,
    length_hbm,
    gains_hbm,
    wq_hbm,
    wk_hbm,
    wv_hbm,
    wo_hbm,
    kc_hbm,
    vc_hbm,
    out_ref,
    layer_ref,
    length_ref,
    gains_ref,
    wq_ref,
    wk_ref,
    wv_ref,
    wo_ref,
    kc_ref,
    vc_ref,
    x_send,
    x_recv,
    p_send,
    p_recv,
    a_send,
    a_recv,
    a_wide,
    y_send,
    y_recv,
    local_sems,
    x_sems,
    p_sems,
    a_sems,
    y_sems,
):
    me = lax.axis_index("gx")
    core = lax.axis_index("gy")
    other = 1 - core
    peers = [lax.rem(me + d, gx) for d in range(1, gx)]
    cols = x_recv.shape[2] - LANES
    kv_local, slots, head = kc_ref.shape
    q_local = wq_ref.shape[1] // head
    group = q_local // kv_local

    barrier = pltpu.get_barrier_semaphore()
    for peer in peers:
        pl.semaphore_signal(barrier, inc=1, device_id={"gx": peer}, device_id_type=MESH)
    pl.semaphore_signal(barrier, inc=1, device_id={"gy": other}, device_id_type=MESH)

    width = wq_ref.shape[1] // kv_local
    depth = wo_ref.shape[0] // OUT_PIECES
    pairs = [(layer_hbm, layer_ref), (length_hbm, length_ref), (gains_hbm, gains_ref)]
    pairs += [(wk_hbm, wk_ref), (wv_hbm, wv_ref)]
    for i in range(kv_local):
        piece = pl.ds(i * width, width)
        pairs.append((wq_hbm.at[:, piece], wq_ref.at[:, piece]))
    pairs += [(kc_hbm.at[0], kc_ref), (vc_hbm.at[0], vc_ref)]
    for i in range(OUT_PIECES):
        piece = pl.ds(i * depth, depth)
        pairs.append((wo_hbm.at[piece], wo_ref.at[piece]))
    loads = [
        pltpu.make_async_copy(src, dst, local_sems.at[i]) for i, (src, dst) in enumerate(pairs)
    ]
    for load in loads:
        load.start()

    def descriptor(src, dst, sems, peer, owner):
        return pltpu.make_async_remote_copy(
            src_ref=src(peer),
            dst_ref=dst(owner),
            send_sem=sems.at[0, peer],
            recv_sem=sems.at[1, owner],
            device_id={"gx": peer},
            device_id_type=MESH,
        )

    def exchange(src, dst, sems):
        copies = [descriptor(src, dst, sems, peer, me) for peer in peers]
        for copy in copies:
            copy.start()
        return copies

    def arrive(src, dst, sems):
        for peer in peers:
            descriptor(src, dst, sems, peer, peer).wait_recv()

    row = hidden_ref[...].astype(jnp.float32)
    inv_row = lax.rsqrt(jnp.mean(row * row, axis=-1, keepdims=True) + 1e-05)
    inv_lanes = jnp.broadcast_to(inv_row, (1, LANES))
    for j in range(gx):
        x_send[j, :, :cols] = row[:, j * cols : (j + 1) * cols]
        x_send[j, :, cols:] = inv_lanes
    x_recv[me] = x_send[me]
    pl.semaphore_wait(barrier, gx)
    x_route = (lambda peer: x_send.at[peer], lambda peer: x_recv.at[peer], x_sems)
    copies = exchange(*x_route)

    half = head // 2
    lane = lax.broadcasted_iota(jnp.int32, (1, head), 1)
    index = jnp.where(lane < half, lane, lane - half).astype(jnp.float32)
    freqs = jnp.exp(-math.log(500000.0) * (index * (2.0 / head)))
    loads[1].wait()
    length = length_ref[0]
    angles = length.astype(jnp.float32) * freqs
    cosine = jnp.cos(angles)
    sine = jnp.sin(angles)
    sine = jnp.where(lane < half, -sine, sine)

    loads[0].wait()
    loads[2].wait()
    table = gains_ref[...].astype(jnp.float32)
    chosen = lax.broadcasted_iota(jnp.int32, table.shape, 0) == layer_ref[0]
    gain = jnp.sum(jnp.where(chosen, table, 0.0), axis=0, keepdims=True)

    arrive(*x_route)
    x32 = x_recv[:, 0, :cols]
    inv = x_recv[:, 0, cols : cols + 1]
    normed = (x32 * inv * gain).astype(jnp.bfloat16)

    def project(weights, first):
        sums = jnp.dot(normed, weights, preferred_element_type=jnp.float32)
        for h in range(sums.shape[1] // head):
            p_send[:, first + h, :] = sums[:, h * head : (h + 1) * head]

    def p_route(first, count, sems):
        rows = pl.ds(first, count)
        return lambda peer: p_send.at[peer, rows], lambda peer: p_recv.at[peer, rows], sems

    def summed_rows(first, count):
        rows = slice(first, first + count)
        total = p_recv[0, rows]
        for j in range(1, gx):
            total = total + p_recv[j, rows]
        return total

    def turn(total):
        return total * cosine + pltpu.roll(total, half, 1) * sine

    early = 2 * kv_local + group
    late = (kv_local - 1) * group
    early_route = p_route(0, early, p_sems.at[0])
    late_route = p_route(early, late, p_sems.at[1])
    loads[3].wait()
    project(wk_ref[...], 0)
    loads[4].wait()
    project(wv_ref[...], kv_local)
    loads[5].wait()
    project(wq_ref[:, :width], 2 * kv_local)
    copies += exchange(*early_route)
    for i in range(1, kv_local):
        loads[5 + i].wait()
        project(wq_ref[:, i * width : (i + 1) * width], 2 * kv_local + i * group)
    copies += exchange(*late_route)
    p_recv[me] = p_send[me]
    loads[5 + kv_local].wait()
    loads[6 + kv_local].wait()
    arrive(*early_route)
    fresh = summed_rows(0, early)
    turned = turn(fresh)

    scale = 1.0 / math.sqrt(head)
    valid = lax.broadcasted_iota(jnp.int32, (1, slots), 1) < length

    def attend(g, rotated):
        rq = rotated.astype(jnp.bfloat16)
        rk = turned[g : g + 1].astype(jnp.bfloat16).astype(jnp.float32)
        nv = fresh[kv_local + g : kv_local + g + 1].astype(jnp.bfloat16).astype(jnp.float32)
        scores = (
            lax.dot_general(
                rq, kc_ref[g], (((1,), (1,)), ((), ())), preferred_element_type=jnp.float32
            )
            * scale
        )
        own = jnp.sum(rq.astype(jnp.float32) * rk, axis=-1, keepdims=True) * scale
        scores = jnp.where(valid, scores, -1e30)
        top = jnp.maximum(jnp.max(scores, axis=-1, keepdims=True), own)
        exps = jnp.where(valid, jnp.exp(scores - top), 0.0)
        own_exp = jnp.exp(own - top)
        denominator = jnp.sum(exps, axis=-1, keepdims=True) + own_exp
        probs = (exps / denominator).astype(jnp.bfloat16)
        own_prob = (own_exp / denominator).astype(jnp.bfloat16).astype(jnp.float32)
        return jnp.dot(probs, vc_ref[g], preferred_element_type=jnp.float32) + own_prob * nv

    attn = [attend(0, turned[2 * kv_local :])]
    arrive(*late_route)
    queries = turn(summed_rows(early, late))
    span = q_local // OUT_PIECES
    groups = kv_local // OUT_PIECES
    a_routes = []
    for i in range(OUT_PIECES):
        while len(attn) < (i + 1) * groups:
            g = len(attn)
            attn.append(attend(g, queries[(g - 1) * group : g * group]))
        piece = jnp.concatenate(attn[i * groups : (i + 1) * groups], axis=0)
        piece = piece.astype(jnp.bfloat16)
        a_send[i] = piece
        route = (
            lambda peer, i=i: a_send.at[i],
            lambda peer, i=i: a_recv.at[i, peer],
            a_sems.at[i],
        )
        copies += exchange(*route)
        a_recv[i, me] = piece
        a_routes.append(route)
    out_width = wo_ref.shape[1] // OUT_PIECES
    total = None
    for i in range(OUT_PIECES):
        loads[7 + kv_local + i].wait()
        arrive(*a_routes[i])
        a_wide[i] = a_recv[i].astype(jnp.float32)
        attended = jnp.concatenate([a_wide[i, :, h, :] for h in range(span)], axis=1)
        attended = attended.astype(jnp.bfloat16)
        rows = slice(i * depth, (i + 1) * depth)
        if i < OUT_PIECES - 1:
            term = jnp.dot(attended, wo_ref[rows], preferred_element_type=jnp.float32)
            total = term if total is None else total + term
    y_copies = []
    for i in range(OUT_PIECES):
        piece = slice(i * out_width, (i + 1) * out_width)
        term = jnp.dot(attended, wo_ref[rows, piece], preferred_element_type=jnp.float32)
        y_send[i] = total[:, piece] + term
        copy = pltpu.make_async_remote_copy(
            src_ref=y_send.at[i],
            dst_ref=y_recv.at[i],
            send_sem=y_sems.at[0, i],
            recv_sem=y_sems.at[1, i],
            device_id={"gy": other},
            device_id_type=MESH,
        )
        copy.start()
        y_copies.append(copy)
    for i in range(OUT_PIECES):
        y_copies[i].wait_recv()
        piece = slice(i * out_width, (i + 1) * out_width)
        summed = y_send[i] + y_recv[i]
        out_ref[:, piece] = (x_recv[:, 0, piece] + summed).astype(out_ref.dtype)
    for copy in copies + y_copies:
        copy.wait_send()


def fused(
    hidden,
    exit_layer,
    norm_gains,
    w_query,
    key_weight,
    value_weight,
    w_out,
    key_cache,
    cached_value_rows,
    lengths,
):
    gx = lax.axis_size("gx")
    cols = norm_gains.shape[1]
    _, kv_local, slots, head = key_cache.shape
    q_local = w_query.shape[1] // head
    heads = q_local + 2 * kv_local
    f32, bf16 = jnp.float32, jnp.bfloat16
    vmem = pl.BlockSpec(memory_space=pltpu.VMEM)
    hbm = pl.BlockSpec(memory_space=pltpu.HBM)
    anywhere = pl.BlockSpec(memory_space=pl.ANY)
    dma = pltpu.SemaphoreType.DMA
    weights = w_query.size + key_weight.size + value_weight.size + w_out.size
    return pl.pallas_call(
        functools.partial(kernel, gx),
        out_shape=jax.ShapeDtypeStruct((gx, cols), bf16),
        in_specs=[vmem, hbm, hbm] + [anywhere] * 7,
        out_specs=vmem,
        scratch_shapes=[
            pltpu.SMEM(exit_layer.shape, jnp.int32),
            pltpu.SMEM(lengths.shape, jnp.int32),
            pltpu.VMEM(norm_gains.shape, bf16),
            pltpu.VMEM(w_query.shape, bf16),
            pltpu.VMEM(key_weight.shape, bf16),
            pltpu.VMEM(value_weight.shape, bf16),
            pltpu.VMEM(w_out.shape, bf16),
            pltpu.VMEM(key_cache.shape[1:], bf16),
            pltpu.VMEM(key_cache.shape[1:], bf16),
            pltpu.VMEM((gx, 1, cols + LANES), f32),
            pltpu.VMEM((gx, 1, cols + LANES), f32),
            pltpu.VMEM((gx, heads, head), f32),
            pltpu.VMEM((gx, heads, head), f32),
            pltpu.VMEM((OUT_PIECES, q_local // OUT_PIECES, head), bf16),
            pltpu.VMEM((OUT_PIECES, gx, q_local // OUT_PIECES, head), bf16),
            pltpu.VMEM((OUT_PIECES, gx, q_local // OUT_PIECES, head), f32),
            pltpu.VMEM((OUT_PIECES, gx, cols // OUT_PIECES), f32),
            pltpu.VMEM((OUT_PIECES, gx, cols // OUT_PIECES), f32),
            dma((7 + kv_local + OUT_PIECES,)),
            dma((2, gx)),
            dma((2, 2, gx)),
            dma((OUT_PIECES, 2, gx)),
            dma((2, OUT_PIECES)),
        ],
        compiler_params=pltpu.CompilerParams(
            collective_id=0, has_side_effects=True, vmem_limit_bytes=56 * 2**20
        ),
        cost_estimate=pl.CostEstimate(
            flops=2 * gx * weights, bytes_accessed=2 * weights, transcendentals=0
        ),
    )(
        hidden,
        exit_layer,
        lengths,
        norm_gains,
        w_query,
        key_weight,
        value_weight,
        w_out,
        key_cache,
        cached_value_rows,
    )


def rotate(vectors, positions):
    half = vectors.shape[-1] // 2
    steps = jnp.arange(half, dtype=jnp.float32) * (2.0 / vectors.shape[-1])
    freqs = jnp.exp(-math.log(500000.0) * steps)
    angles = positions[:, None, None] * freqs[None, None, :]
    cosine = jnp.cos(angles)
    sine = jnp.sin(angles)
    first = vectors[..., :half]
    second = vectors[..., half:]
    return jnp.concatenate(
        [first * cosine - second * sine, second * cosine + first * sine], axis=-1
    )


def body(
    hidden,
    exit_layer,
    norm_gains,
    w_query,
    key_weight,
    value_weight,
    w_out,
    key_cache,
    cached_value_rows,
    lengths,
):
    rows_dev = hidden.shape[0]
    head = key_cache.shape[3]
    kv_local = key_cache.shape[1]
    q_local = w_query.shape[1] // head
    group = q_local // kv_local
    columns = lax.all_to_all(hidden, "gx", split_axis=1, concat_axis=0, tiled=True)
    x32 = columns.astype(jnp.float32)
    own_rows = hidden.astype(jnp.float32)
    inv_local = lax.rsqrt(jnp.mean(own_rows * own_rows, axis=-1) + 1e-05)
    inv = lax.all_gather(inv_local, "gx", axis=0, tiled=True)
    gain = lax.dynamic_index_in_dim(norm_gains, exit_layer[0], 0, keepdims=False).astype(
        jnp.float32
    )
    normed = (x32 * inv[:, None] * gain[None, :]).astype(jnp.bfloat16)
    weights = jnp.concatenate([w_query, key_weight, value_weight], axis=1)
    width_q = w_query.shape[1]
    width_k = key_weight.shape[1]
    partial_sums = jnp.dot(normed, weights, preferred_element_type=jnp.float32)
    shares = lax.psum_scatter(partial_sums, "gx", scatter_dimension=1, tiled=True)
    projected = lax.all_to_all(shares, "gx", split_axis=0, concat_axis=1, tiled=True)
    query = projected[:, :width_q]
    keys = projected[:, width_q : width_q + width_k]
    values = projected[:, width_q + width_k :]
    positions = lengths.astype(jnp.float32)
    rq = rotate(query.reshape(rows_dev, q_local, head), positions).astype(jnp.bfloat16)
    rk = rotate(keys.reshape(rows_dev, kv_local, head), positions).astype(jnp.bfloat16)
    nv = values.reshape(rows_dev, kv_local, head).astype(jnp.bfloat16)
    scale = 1.0 / math.sqrt(head)
    grouped = rq.reshape(rows_dev, kv_local, group, head)
    scores = (
        jnp.einsum("rgqd,rgpd->rgqp", grouped, key_cache, preferred_element_type=jnp.float32)
        * scale
    )
    own = jnp.einsum("rgqd,rgd->rgq", grouped, rk, preferred_element_type=jnp.float32) * scale
    valid = jnp.arange(key_cache.shape[2], dtype=jnp.int32)[None, :] < lengths[:, None]
    scores = jnp.where(valid[:, None, None, :], scores, -1e30)
    top = jnp.maximum(jnp.max(scores, axis=-1), own)
    weights_exp = jnp.where(valid[:, None, None, :], jnp.exp(scores - top[..., None]), 0.0)
    own_weight = jnp.exp(own - top)
    total = jnp.sum(weights_exp, axis=-1) + own_weight
    probs = (weights_exp / total[..., None]).astype(jnp.bfloat16)
    own_prob = (own_weight / total).astype(jnp.bfloat16)
    attn = jnp.einsum(
        "rgqp,rgpd->rgqd", probs, cached_value_rows, preferred_element_type=jnp.float32
    )
    attn = attn + own_prob.astype(jnp.float32)[..., None] * nv.astype(jnp.float32)[:, :, None, :]
    attn = attn.reshape(rows_dev, q_local * head).astype(jnp.bfloat16)
    mixed = jnp.dot(
        lax.all_gather(attn, "gx", axis=0, tiled=True), w_out, preferred_element_type=jnp.float32
    )
    summed = lax.psum(mixed, "gy")
    return (x32 + summed).astype(jnp.bfloat16)


def step(*arrays):
    hidden, gains = arrays[0], arrays[2]
    if gains.shape[1] % (LANES * OUT_PIECES) == 0 and hidden.shape[0] == 1:
        return fused(*arrays)
    return body(*arrays)


def solution(mesh):
    placed = (
        P(("replica", "gx"), None),
        P("replica"),
        P(None, "gx"),
        P("gx", "gy"),
        P("gx", "gy"),
        P("gx", "gy"),
        P("gy", "gx"),
        P(("replica", "gx"), "gy", None, None),
        P(("replica", "gx"), "gy", None, None),
        P(("replica", "gx")),
    )
    return jax.shard_map(
        step, mesh=mesh, in_specs=placed, out_specs=P("replica", "gx"), check_vma=False
    )
```

```python
import functools
import math

import jax
import jax.numpy as jnp
from jax import lax
from jax.experimental import pallas as pl
from jax.experimental.pallas import tpu as pltpu
from jax.sharding import PartitionSpec as P

MESH = pl.DeviceIdType.MESH
LANES = 128
OUT_PIECES = 2


def kernel(
    gx,
    hidden_ref,
    layer_hbm,
    length_hbm,
    gains_hbm,
    wq_hbm,
    wk_hbm,
    wv_hbm,
    wo_hbm,
    kc_hbm,
    vc_hbm,
    out_ref,
    layer_ref,
    length_ref,
    gains_ref,
    wq_ref,
    wk_ref,
    wv_ref,
    wo_ref,
    kc_ref,
    vc_ref,
    x_send,
    x_recv,
    p_send,
    p_recv,
    a_send,
    a_recv,
    a_wide,
    y_send,
    y_recv,
    local_sems,
    x_sems,
    p_sems,
    a_sems,
    y_sems,
):
    me = lax.axis_index("gx")
    core = lax.axis_index("gy")
    other = 1 - core
    peers = [lax.rem(me + d, gx) for d in range(1, gx)]
    cols = x_recv.shape[2] - LANES
    kv_local, slots, head = kc_ref.shape
    q_local = wq_ref.shape[1] // head
    group = q_local // kv_local

    barrier = pltpu.get_barrier_semaphore()
    for peer in peers:
        pl.semaphore_signal(barrier, inc=1, device_id={"gx": peer}, device_id_type=MESH)
    pl.semaphore_signal(barrier, inc=1, device_id={"gy": other}, device_id_type=MESH)

    width = wq_ref.shape[1] // kv_local
    depth = wo_ref.shape[0] // OUT_PIECES
    pairs = [(layer_hbm, layer_ref), (length_hbm, length_ref), (gains_hbm, gains_ref)]
    pairs += [(wk_hbm, wk_ref), (wv_hbm, wv_ref)]
    for i in range(kv_local):
        piece = pl.ds(i * width, width)
        pairs.append((wq_hbm.at[:, piece], wq_ref.at[:, piece]))
    pairs += [(kc_hbm.at[0], kc_ref), (vc_hbm.at[0], vc_ref)]
    for i in range(OUT_PIECES):
        piece = pl.ds(i * depth, depth)
        pairs.append((wo_hbm.at[piece], wo_ref.at[piece]))
    loads = [
        pltpu.make_async_copy(src, dst, local_sems.at[i]) for i, (src, dst) in enumerate(pairs)
    ]
    for load in loads[: 5 + kv_local]:
        load.start()

    def descriptor(src, dst, sems, peer, owner):
        return pltpu.make_async_remote_copy(
            src_ref=src(peer),
            dst_ref=dst(owner),
            send_sem=sems.at[0, peer],
            recv_sem=sems.at[1, owner],
            device_id={"gx": peer},
            device_id_type=MESH,
        )

    def exchange(src, dst, sems):
        copies = [descriptor(src, dst, sems, peer, me) for peer in peers]
        for copy in copies:
            copy.start()
        return copies

    def arrive(src, dst, sems):
        for peer in peers:
            descriptor(src, dst, sems, peer, peer).wait_recv()

    row = hidden_ref[...].astype(jnp.float32)
    inv_row = lax.rsqrt(jnp.mean(row * row, axis=-1, keepdims=True) + 1e-05)
    inv_lanes = jnp.broadcast_to(inv_row, (1, LANES))
    for j in range(gx):
        x_send[j, :, :cols] = row[:, j * cols : (j + 1) * cols]
        x_send[j, :, cols:] = inv_lanes
    x_recv[me] = x_send[me]
    pl.semaphore_wait(barrier, gx)
    x_route = (lambda peer: x_send.at[peer], lambda peer: x_recv.at[peer], x_sems)
    copies = exchange(*x_route)
    for load in loads[5 + kv_local :]:
        load.start()

    half = head // 2
    lane = lax.broadcasted_iota(jnp.int32, (1, head), 1)
    index = jnp.where(lane < half, lane, lane - half).astype(jnp.float32)
    freqs = jnp.exp(-math.log(500000.0) * (index * (2.0 / head)))
    loads[1].wait()
    length = length_ref[0]
    angles = length.astype(jnp.float32) * freqs
    cosine = jnp.cos(angles)
    sine = jnp.sin(angles)
    sine = jnp.where(lane < half, -sine, sine)

    loads[0].wait()
    loads[2].wait()
    table = gains_ref[...].astype(jnp.float32)
    chosen = lax.broadcasted_iota(jnp.int32, table.shape, 0) == layer_ref[0]
    gain = jnp.sum(jnp.where(chosen, table, 0.0), axis=0, keepdims=True)

    arrive(*x_route)
    x32 = x_recv[:, 0, :cols]
    inv = x_recv[:, 0, cols : cols + 1]
    normed = (x32 * inv * gain).astype(jnp.bfloat16)

    def project(weights, first):
        sums = jnp.dot(normed, weights, preferred_element_type=jnp.float32)
        for h in range(sums.shape[1] // head):
            p_send[:, first + h, :] = sums[:, h * head : (h + 1) * head]

    def p_route(first, count, sems):
        rows = pl.ds(first, count)
        return lambda peer: p_send.at[peer, rows], lambda peer: p_recv.at[peer, rows], sems

    def summed_rows(first, count):
        rows = slice(first, first + count)
        total = p_recv[0, rows]
        for j in range(1, gx):
            total = total + p_recv[j, rows]
        return total

    def turn(total):
        return total * cosine + pltpu.roll(total, half, 1) * sine

    early = 2 * kv_local + group
    late = (kv_local - 1) * group
    early_route = p_route(0, early, p_sems.at[0])
    late_route = p_route(early, late, p_sems.at[1])
    loads[3].wait()
    project(wk_ref[...], 0)
    loads[4].wait()
    project(wv_ref[...], kv_local)
    loads[5].wait()
    project(wq_ref[:, :width], 2 * kv_local)
    copies += exchange(*early_route)
    for i in range(1, kv_local):
        loads[5 + i].wait()
        project(wq_ref[:, i * width : (i + 1) * width], 2 * kv_local + i * group)
    copies += exchange(*late_route)
    p_recv[me] = p_send[me]
    loads[5 + kv_local].wait()
    loads[6 + kv_local].wait()
    arrive(*early_route)
    fresh = summed_rows(0, early)
    turned = turn(fresh)

    scale = 1.0 / math.sqrt(head)
    valid = lax.broadcasted_iota(jnp.int32, (1, slots), 1) < length

    def attend(g, rotated):
        rq = rotated.astype(jnp.bfloat16)
        rk = turned[g : g + 1].astype(jnp.bfloat16).astype(jnp.float32)
        nv = fresh[kv_local + g : kv_local + g + 1].astype(jnp.bfloat16).astype(jnp.float32)
        scores = (
            lax.dot_general(
                rq, kc_ref[g], (((1,), (1,)), ((), ())), preferred_element_type=jnp.float32
            )
            * scale
        )
        own = jnp.sum(rq.astype(jnp.float32) * rk, axis=-1, keepdims=True) * scale
        scores = jnp.where(valid, scores, -1e30)
        top = jnp.maximum(jnp.max(scores, axis=-1, keepdims=True), own)
        exps = jnp.where(valid, jnp.exp(scores - top), 0.0)
        own_exp = jnp.exp(own - top)
        denominator = jnp.sum(exps, axis=-1, keepdims=True) + own_exp
        probs = (exps / denominator).astype(jnp.bfloat16)
        own_prob = (own_exp / denominator).astype(jnp.bfloat16).astype(jnp.float32)
        return jnp.dot(probs, vc_ref[g], preferred_element_type=jnp.float32) + own_prob * nv

    attn = [attend(0, turned[2 * kv_local :])]
    arrive(*late_route)
    queries = turn(summed_rows(early, late))
    span = q_local // OUT_PIECES
    groups = kv_local // OUT_PIECES
    a_routes = []
    for i in range(OUT_PIECES):
        while len(attn) < (i + 1) * groups:
            g = len(attn)
            attn.append(attend(g, queries[(g - 1) * group : g * group]))
        piece = jnp.concatenate(attn[i * groups : (i + 1) * groups], axis=0)
        piece = piece.astype(jnp.bfloat16)
        a_send[i] = piece
        route = (
            lambda peer, i=i: a_send.at[i],
            lambda peer, i=i: a_recv.at[i, peer],
            a_sems.at[i],
        )
        copies += exchange(*route)
        a_recv[i, me] = piece
        a_routes.append(route)
    out_width = wo_ref.shape[1] // OUT_PIECES
    total = None
    for i in range(OUT_PIECES):
        loads[7 + kv_local + i].wait()
        arrive(*a_routes[i])
        a_wide[i] = a_recv[i].astype(jnp.float32)
        attended = jnp.concatenate([a_wide[i, :, h, :] for h in range(span)], axis=1)
        attended = attended.astype(jnp.bfloat16)
        rows = slice(i * depth, (i + 1) * depth)
        if i < OUT_PIECES - 1:
            term = jnp.dot(attended, wo_ref[rows], preferred_element_type=jnp.float32)
            total = term if total is None else total + term
    y_copies = []
    for i in range(OUT_PIECES):
        piece = slice(i * out_width, (i + 1) * out_width)
        term = jnp.dot(attended, wo_ref[rows, piece], preferred_element_type=jnp.float32)
        y_send[i] = total[:, piece] + term
        copy = pltpu.make_async_remote_copy(
            src_ref=y_send.at[i],
            dst_ref=y_recv.at[i],
            send_sem=y_sems.at[0, i],
            recv_sem=y_sems.at[1, i],
            device_id={"gy": other},
            device_id_type=MESH,
        )
        copy.start()
        y_copies.append(copy)
    for i in range(OUT_PIECES):
        y_copies[i].wait_recv()
        piece = slice(i * out_width, (i + 1) * out_width)
        summed = y_send[i] + y_recv[i]
        out_ref[:, piece] = (x_recv[:, 0, piece] + summed).astype(out_ref.dtype)
    for copy in copies + y_copies:
        copy.wait_send()


def fused(
    hidden,
    exit_layer,
    norm_gains,
    w_query,
    key_weight,
    value_weight,
    w_out,
    key_cache,
    cached_value_rows,
    lengths,
):
    gx = lax.axis_size("gx")
    cols = norm_gains.shape[1]
    _, kv_local, slots, head = key_cache.shape
    q_local = w_query.shape[1] // head
    heads = q_local + 2 * kv_local
    f32, bf16 = jnp.float32, jnp.bfloat16
    vmem = pl.BlockSpec(memory_space=pltpu.VMEM)
    hbm = pl.BlockSpec(memory_space=pltpu.HBM)
    anywhere = pl.BlockSpec(memory_space=pl.ANY)
    dma = pltpu.SemaphoreType.DMA
    weights = w_query.size + key_weight.size + value_weight.size + w_out.size
    return pl.pallas_call(
        functools.partial(kernel, gx),
        out_shape=jax.ShapeDtypeStruct((gx, cols), bf16),
        in_specs=[vmem, hbm, hbm] + [anywhere] * 7,
        out_specs=vmem,
        scratch_shapes=[
            pltpu.SMEM(exit_layer.shape, jnp.int32),
            pltpu.SMEM(lengths.shape, jnp.int32),
            pltpu.VMEM(norm_gains.shape, bf16),
            pltpu.VMEM(w_query.shape, bf16),
            pltpu.VMEM(key_weight.shape, bf16),
            pltpu.VMEM(value_weight.shape, bf16),
            pltpu.VMEM(w_out.shape, bf16),
            pltpu.VMEM(key_cache.shape[1:], bf16),
            pltpu.VMEM(key_cache.shape[1:], bf16),
            pltpu.VMEM((gx, 1, cols + LANES), f32),
            pltpu.VMEM((gx, 1, cols + LANES), f32),
            pltpu.VMEM((gx, heads, head), f32),
            pltpu.VMEM((gx, heads, head), f32),
            pltpu.VMEM((OUT_PIECES, q_local // OUT_PIECES, head), bf16),
            pltpu.VMEM((OUT_PIECES, gx, q_local // OUT_PIECES, head), bf16),
            pltpu.VMEM((OUT_PIECES, gx, q_local // OUT_PIECES, head), f32),
            pltpu.VMEM((OUT_PIECES, gx, cols // OUT_PIECES), f32),
            pltpu.VMEM((OUT_PIECES, gx, cols // OUT_PIECES), f32),
            dma((7 + kv_local + OUT_PIECES,)),
            dma((2, gx)),
            dma((2, 2, gx)),
            dma((OUT_PIECES, 2, gx)),
            dma((2, OUT_PIECES)),
        ],
        compiler_params=pltpu.CompilerParams(
            collective_id=0, has_side_effects=True, vmem_limit_bytes=56 * 2**20
        ),
        cost_estimate=pl.CostEstimate(
            flops=2 * gx * weights, bytes_accessed=2 * weights, transcendentals=0
        ),
    )(
        hidden,
        exit_layer,
        lengths,
        norm_gains,
        w_query,
        key_weight,
        value_weight,
        w_out,
        key_cache,
        cached_value_rows,
    )


def rotate(vectors, positions):
    half = vectors.shape[-1] // 2
    steps = jnp.arange(half, dtype=jnp.float32) * (2.0 / vectors.shape[-1])
    freqs = jnp.exp(-math.log(500000.0) * steps)
    angles = positions[:, None, None] * freqs[None, None, :]
    cosine = jnp.cos(angles)
    sine = jnp.sin(angles)
    first = vectors[..., :half]
    second = vectors[..., half:]
    return jnp.concatenate(
        [first * cosine - second * sine, second * cosine + first * sine], axis=-1
    )


def body(
    hidden,
    exit_layer,
    norm_gains,
    w_query,
    key_weight,
    value_weight,
    w_out,
    key_cache,
    cached_value_rows,
    lengths,
):
    rows_dev = hidden.shape[0]
    head = key_cache.shape[3]
    kv_local = key_cache.shape[1]
    q_local = w_query.shape[1] // head
    group = q_local // kv_local
    columns = lax.all_to_all(hidden, "gx", split_axis=1, concat_axis=0, tiled=True)
    x32 = columns.astype(jnp.float32)
    own_rows = hidden.astype(jnp.float32)
    inv_local = lax.rsqrt(jnp.mean(own_rows * own_rows, axis=-1) + 1e-05)
    inv = lax.all_gather(inv_local, "gx", axis=0, tiled=True)
    gain = lax.dynamic_index_in_dim(norm_gains, exit_layer[0], 0, keepdims=False).astype(
        jnp.float32
    )
    normed = (x32 * inv[:, None] * gain[None, :]).astype(jnp.bfloat16)
    weights = jnp.concatenate([w_query, key_weight, value_weight], axis=1)
    width_q = w_query.shape[1]
    width_k = key_weight.shape[1]
    partial_sums = jnp.dot(normed, weights, preferred_element_type=jnp.float32)
    shares = lax.psum_scatter(partial_sums, "gx", scatter_dimension=1, tiled=True)
    projected = lax.all_to_all(shares, "gx", split_axis=0, concat_axis=1, tiled=True)
    query = projected[:, :width_q]
    keys = projected[:, width_q : width_q + width_k]
    values = projected[:, width_q + width_k :]
    positions = lengths.astype(jnp.float32)
    rq = rotate(query.reshape(rows_dev, q_local, head), positions).astype(jnp.bfloat16)
    rk = rotate(keys.reshape(rows_dev, kv_local, head), positions).astype(jnp.bfloat16)
    nv = values.reshape(rows_dev, kv_local, head).astype(jnp.bfloat16)
    scale = 1.0 / math.sqrt(head)
    grouped = rq.reshape(rows_dev, kv_local, group, head)
    scores = (
        jnp.einsum("rgqd,rgpd->rgqp", grouped, key_cache, preferred_element_type=jnp.float32)
        * scale
    )
    own = jnp.einsum("rgqd,rgd->rgq", grouped, rk, preferred_element_type=jnp.float32) * scale
    valid = jnp.arange(key_cache.shape[2], dtype=jnp.int32)[None, :] < lengths[:, None]
    scores = jnp.where(valid[:, None, None, :], scores, -1e30)
    top = jnp.maximum(jnp.max(scores, axis=-1), own)
    weights_exp = jnp.where(valid[:, None, None, :], jnp.exp(scores - top[..., None]), 0.0)
    own_weight = jnp.exp(own - top)
    total = jnp.sum(weights_exp, axis=-1) + own_weight
    probs = (weights_exp / total[..., None]).astype(jnp.bfloat16)
    own_prob = (own_weight / total).astype(jnp.bfloat16)
    attn = jnp.einsum(
        "rgqp,rgpd->rgqd", probs, cached_value_rows, preferred_element_type=jnp.float32
    )
    attn = attn + own_prob.astype(jnp.float32)[..., None] * nv.astype(jnp.float32)[:, :, None, :]
    attn = attn.reshape(rows_dev, q_local * head).astype(jnp.bfloat16)
    mixed = jnp.dot(
        lax.all_gather(attn, "gx", axis=0, tiled=True), w_out, preferred_element_type=jnp.float32
    )
    summed = lax.psum(mixed, "gy")
    return (x32 + summed).astype(jnp.bfloat16)


def step(*arrays):
    hidden, gains = arrays[0], arrays[2]
    if gains.shape[1] % (LANES * OUT_PIECES) == 0 and hidden.shape[0] == 1:
        return fused(*arrays)
    return body(*arrays)


def solution(mesh):
    placed = (
        P(("replica", "gx"), None),
        P("replica"),
        P(None, "gx"),
        P("gx", "gy"),
        P("gx", "gy"),
        P("gx", "gy"),
        P("gy", "gx"),
        P(("replica", "gx"), "gy", None, None),
        P(("replica", "gx"), "gy", None, None),
        P(("replica", "gx")),
    )
    return jax.shard_map(
        step, mesh=mesh, in_specs=placed, out_specs=P("replica", "gx"), check_vma=False
    )
```
